32 devices in a mesh: groups: 2 (over x), wide: 8 (over z, y), narrow: 2 (over core).
Axes of the slice: x: 2, y: 2, z: 4, core: 2. Of those that a mesh axis runs over, the one named last changes fastest.
Arguments:
- activations: bfloat16 [256, 5120], P(('groups', 'narrow'), 'wide'), parts along dimension 0, may hold values from -6 to 6
- out_grads: bfloat16 [256, 25600], P(('groups', 'wide'), 'narrow'), parts along dimension 0, may hold values from -0.029907227 to 0.029907227
- second_moment: float32 [5120, 25600], P('wide', 'narrow'), may hold values from 0.0001 to 0.01
- seq_ids: int32 [256], P('groups'), parts along dimension 0, may hold values from 0 to 1, never falling along the last dimension, each value on 1 to 96 neighbouring positions
- seed_word: int32 [1], replicated, may hold values from 0 to 1073741823
- row_keys: int32 [5120], P('wide'), may hold values from 0 to 1073741823
- col_keys: int32 [25600], P('narrow'), may hold values from 0 to 1073741823
Outputs:
- features: float32 [4, 1024], P('groups'), parts along dimension 0
The draws below stay inside these ranges and needn't reach their ends.
There are 2 independent parts, one for each index of `groups`. The reference program is written for one: setup_inputs(seed, part) draws one part's arguments, and reference() takes and returns one part's arrays. A program takes and returns all parts, laid end to end along the dimension named above; an argument that names none is the same for every part. Nothing has to cross between parts.
Inputs may be any that keep to these rules, and one draw needn't show every extreme that they name: `seq_ids`: tokens of one sequence stand together, sequence numbers never fall along the tokens, and every sequence has at least one token.
All inputs are finite; a program needn't handle non-finite values.
Results may differ from the reference program's by a relative error of at most 0.0029.
Values may be sent and summed in bfloat16 or wider, within the bound.
A program may use at most 192 MiB of HBM per device.

```python
import math
import jax
import jax.numpy as jnp
import numpy as np
from jax import lax

D = 5120
FF = 25600
K = 1024
SEQS = 2
TOKENS = 128
MOST = 96


def place_ends(result, own_key, smallest, high):
    longest = result.shape.index(max(result.shape))
    spots = []
    for shift in (0, 1):
        where = [jax.random.randint(jax.random.fold_in(own_key, axis), (), 0, length) for axis, length in enumerate(result.shape)]
        where[longest] = (where[longest] + shift) % result.shape[longest]
        spots.append(tuple(where))
    return result.at[spots[0]].set(smallest).at[spots[1]].set(high)


def steps_of(key, shape, pieces, low, high):
    loudness, own = 1.0, jax.random.fold_in(key, 6)
    for position, parts in pieces:
        draws = jnp.exp(jax.random.uniform(jax.random.fold_in(own, position), (parts,), jnp.float32, low / len(pieces), high / len(pieces)))
        loudness = loudness * jnp.repeat(draws, shape[position] // parts).reshape([-1 if axis == position else 1 for axis in range(len(shape))])
    return loudness


def split_up(number_of, total, most, lean):
    loads = [(1 << 20) // math.isqrt(rank ** lean) + 1 for rank in range(2, number_of + 1)]
    spare, counts = total - most - (number_of - 1), [1] * (number_of - 1)
    while spare > 0:
        movable = [i for i in range(number_of - 1) if counts[i] < most]
        whole, budget = sum([loads[i] for i in movable]), spare
        for i in movable:
            extra = min(most - counts[i], max(1, budget * loads[i] // whole), spare)
            counts[i] = counts[i] + extra
            spare = spare - extra
    return np.array([most] + counts)


def uneven_parts(stream_key, count, total, reach, slope):
    if count == 2:
        one = jax.random.randint(stream_key, (), max(1, total - reach), min(reach, total - 1) + 1)
        return jnp.stack([one, total - one])
    sizes = jnp.asarray(split_up(count, total, reach, slope), jnp.int32)
    pairs = (count - 1) // 2
    donor, taker = sizes[1:1 + 2 * pairs:2], sizes[2:2 + 2 * pairs:2]
    room = jnp.minimum(donor - 1, reach - taker)
    moved = jax.random.randint(jax.random.fold_in(stream_key, 1), (pairs,), 0, 1 << 20) % (room + 1)
    sizes = sizes.at[1:1 + 2 * pairs:2].set(donor - moved).at[2:2 + 2 * pairs:2].set(taker + moved)
    return sizes[jax.random.permutation(jax.random.fold_in(stream_key, 2), count)]


def centred(stream_key, dims, deviation, bound, shards=(), held_as=jnp.bfloat16):
    result = jax.random.normal(stream_key, dims, jnp.float32) * deviation
    if len(shards) > 0:
        result = steps_of(stream_key, dims, shards, -0.22, 0.18) * result
    return jnp.clip(result, min=-bound, max=bound).astype(held_as)


def setup_inputs(seed: int = 0, part: int = 0) -> dict:
    streams_of = jax.random.split(jax.random.key(seed), 8)
    part_keys = jax.random.split(jax.random.fold_in(streams_of[7], part), 8)
    return {
        "activations": centred(part_keys[0], (TOKENS, D), 1.0, 6.0, ((0, 2), (1, 8))),
        "out_grads": centred(part_keys[1], (TOKENS, FF), 0.005, 0.029907227, ((0, 8), (1, 2))),
        "second_moment": jnp.clip(jnp.exp(math.log(0.01) - 4.6051702 * jax.random.uniform(streams_of[2], (D, FF), jnp.float32) ** steps_of(streams_of[2], (D, FF), ((0, 8), (1, 2)), -0.2, 0.2)), 0.0001, 0.01),
        "seq_ids": jnp.searchsorted(jnp.cumsum(uneven_parts(part_keys[3], SEQS, TOKENS, MOST, 0)), jnp.arange(TOKENS), side="right").astype(jnp.int32),
        "seed_word": jax.random.randint(streams_of[4], (1,), 0, 1073741824).astype(jnp.int32),
        "row_keys": place_ends(jax.random.randint(streams_of[5], (D,), 0, 1073741824), jax.random.fold_in(streams_of[5], 1), 0, 1073741823).astype(jnp.int32),
        "col_keys": place_ends(jax.random.randint(streams_of[6], (FF,), 0, 1073741824), jax.random.fold_in(streams_of[6], 1), 0, 1073741823).astype(jnp.int32),
    }


adam_epsilon = 1e-08

def scramble(number):
    number = number * 668265261
    number = number ^ lax.shift_right_logical(number, jnp.full_like(number, 15))
    number = number * 739982445
    number = number ^ lax.shift_right_logical(number, jnp.full_like(number, 13))
    number = number * 695872825
    return number ^ lax.shift_right_logical(number, jnp.full_like(number, 16))

def rademacher(key_list, seed_word, salt_value, count_cols):
    salted = scramble(key_list ^ seed_word[0] + salt_value)
    columns = lax.broadcasted_iota(jnp.int32, (key_list.shape[0], count_cols), 1)
    hashed = scramble(salted[:, None] ^ scramble(columns + salt_value))
    parity = lax.shift_right_logical(hashed, jnp.full_like(hashed, 20)) & 1
    return (1 - 2 * parity).astype(jnp.float32)

def reference(activations, out_grads, second_moment, seq_ids, seed_word, row_keys, col_keys):
    row_signs = rademacher(row_keys, seed_word, 1, K)
    col_signs = rademacher(col_keys, seed_word, 2, K).astype(jnp.bfloat16)
    precond = 1.0 / (jnp.sqrt(second_moment) + adam_epsilon)
    norm_factor = 1.0 / jnp.sqrt(jnp.float32(D) * jnp.float32(FF))
    results = []
    for segment in range(SEQS):
        picked = jnp.where((seq_ids == segment)[:, None], activations, jnp.zeros_like(activations))
        grad = jnp.dot(picked.T, out_grads, preferred_element_type=jnp.float32)
        scaled = (grad * precond).astype(jnp.bfloat16)
        mapped = jnp.dot(scaled, col_signs, preferred_element_type=jnp.float32)
        results.append(lax.optimization_barrier(jnp.sum(mapped * row_signs, axis=0)) * norm_factor)
    return jnp.stack(results)
```

```python
import functools

import jax
import jax.numpy as jnp
from jax import lax
from jax.experimental import pallas as pl
from jax.experimental.pallas import tpu as pltpu
from jax.sharding import PartitionSpec as P

D = 5120
FF = 25600
K = 1024
SEQS = 2

adam_epsilon = 1e-08
PIECES = (1, 2, 2)


def scramble_start(number):
    number = number * 668265261
    number = number ^ lax.shift_right_logical(number, jnp.full_like(number, 15))
    number = number * 739982445
    return number ^ lax.shift_right_logical(number, jnp.full_like(number, 13))


def scramble(number):
    number = scramble_start(number) * 695872825
    return number ^ lax.shift_right_logical(number, jnp.full_like(number, 16))


LAST = ((695872825 << 11) + (1 << 31)) % (1 << 32) - (1 << 31)


def signs_of(salted, lanes):
    mixed = scramble_start(salted ^ lanes) * LAST
    return jnp.where(mixed < 0, jnp.float32(-1.0), jnp.float32(1.0))


def prepare_kernel(first_ref, salted_ref, lanes_ref, moment_ref, signs_ref, precond_ref, *, step):
    def hash_rows(i, carry):
        rows = pl.ds(pl.multiple_of(i * step, step), step)
        signs_ref[rows, :] = signs_of(salted_ref[rows, :], lanes_ref[...]).astype(jnp.bfloat16)
        return carry

    lax.fori_loop(0, signs_ref.shape[0] // step, hash_rows, 0)

    def moment_rows(i, carry):
        rows = pl.ds(pl.multiple_of(i * 8, 8), 8)
        precond_ref[rows, :] = 1.0 / (jnp.sqrt(moment_ref[rows, :]) + adam_epsilon)
        return carry

    lax.fori_loop(0, moment_ref.shape[0] // 8, moment_rows, 0)


def map_kernel(picked_ref, dy_ref, precond_ref, signs_ref, salted_ref, lanes_ref, out_ref, rows_ref):
    rows = precond_ref.shape[0]

    @pl.when(pl.program_id(0) == 0)
    def _():
        out_ref[...] = jnp.zeros_like(out_ref)

        def hash_rows(i, carry):
            part = pl.ds(pl.multiple_of(i * 8, 8), 8)
            rows_ref[part, :] = signs_of(salted_ref[part, :], lanes_ref[...])
            return carry

        lax.fori_loop(0, rows // 8, hash_rows, 0)

    for s in range(picked_ref.shape[0]):
        grad = jnp.dot(picked_ref[s], dy_ref[...], preferred_element_type=jnp.float32)
        scaled = (grad * precond_ref[...]).astype(jnp.bfloat16)
        mapped = jnp.dot(scaled, signs_ref[...], preferred_element_type=jnp.float32)
        out_ref[s : s + 1, :] += jnp.sum(mapped * rows_ref[...], axis=0, keepdims=True)


def on_device(activations, out_grads, second_moment, seq_ids, seed_word, row_keys, col_keys):
    groups = lax.axis_size("groups")
    wide = lax.axis_size("wide")
    me = lax.axis_index("groups")
    rows, all_cols = second_moment.shape
    cols = all_cols // groups
    tokens = seq_ids.shape[0]
    per = out_grads.shape[0]
    chunk = 1280 if cols % 1280 == 0 else 640
    count = cols // chunk

    with jax.named_scope("exchange"):
        parts = [lax.dynamic_slice_in_dim(out_grads, me * cols, cols, axis=1)]
        for shift in range(1, groups):
            target = lax.rem(me + shift, groups)
            block = lax.dynamic_slice_in_dim(out_grads, target * cols, cols, axis=1)
            parts.append(lax.ppermute(block, "groups", [(i, (i + shift) % groups) for i in range(groups)]))
        mine = jnp.concatenate(parts, axis=0)

    pieces, start = [], 0
    for size in PIECES:
        if start < count:
            pieces.append((start, min(size, count - start)))
            start += size
    if start < count:
        pieces.append((start, count - start))

    gathered = []
    for at, size in pieces:
        piece = mine[:, at * chunk : (at + size) * chunk]
        gathered.append(lax.all_gather(piece, "wide", axis=0, tiled=True))

    with jax.named_scope("masked_activations"):
        whole_x = lax.all_gather(activations, ("groups", "narrow"), axis=0, tiled=True)
        ids = lax.all_gather(seq_ids, "groups", axis=0, tiled=True).reshape(groups, wide, per)
        order = lax.rem(me + groups - jnp.arange(groups), groups)
        x = jnp.take(whole_x.reshape(groups, wide, per, rows), order, axis=0)
        ids = jnp.take(ids, order, axis=0)
        x = x.transpose(3, 1, 0, 2).reshape(rows, groups * tokens)
        which = ids + SEQS * jnp.arange(groups, dtype=jnp.int32)[:, None, None]
        which = which.transpose(1, 0, 2).reshape(groups * tokens)
        mask = which[None, :] == jnp.arange(groups * SEQS, dtype=jnp.int32)[:, None]
        picked = jnp.where(mask[:, None, :], x[None], jnp.zeros_like(x)[None])

    seed = seed_word[0]
    lane = jnp.arange(K, dtype=jnp.int32)[None, :]
    row_salted = scramble(row_keys ^ (seed + 1))[:, None]
    my_keys = lax.dynamic_slice_in_dim(col_keys, me * cols, cols)
    col_salted = scramble(my_keys ^ (seed + 2))[:, None]
    row_lanes = scramble(lane + 1)
    col_lanes = scramble(lane + 2)

    signs, precond = pl.pallas_call(
        functools.partial(prepare_kernel, step=16),
        grid_spec=pltpu.PrefetchScalarGridSpec(
            num_scalar_prefetch=1,
            grid=(count,),
            in_specs=[
                pl.BlockSpec((chunk, 1), lambda i, f: (i, 0)),
                pl.BlockSpec((1, K), lambda i, f: (0, 0)),
                pl.BlockSpec((rows, chunk), lambda i, f: (0, f[0] + i)),
            ],
            out_specs=[
                pl.BlockSpec((chunk, K), lambda i, f: (i, 0)),
                pl.BlockSpec((rows, chunk), lambda i, f: (0, i)),
            ],
        ),
        out_shape=[
            jax.ShapeDtypeStruct((cols, K), jnp.bfloat16),
            jax.ShapeDtypeStruct((rows, cols), jnp.float32),
        ],
        compiler_params=pltpu.CompilerParams(vmem_limit_bytes=40 << 20),
        cost_estimate=pl.CostEstimate(flops=cols * K * 20, bytes_accessed=rows * cols * 8 + cols * K * 2, transcendentals=2 * rows * cols),
        name="prepare",
    )((me * count).astype(jnp.int32).reshape(1), col_salted, col_lanes, second_moment)

    total = jnp.zeros((groups * SEQS, K), jnp.float32)
    for (at, size), dy in zip(pieces, gathered):
        total = total + pl.pallas_call(
            map_kernel,
            grid=(size,),
            in_specs=[
                pl.BlockSpec(picked.shape, lambda i: (0, 0, 0)),
                pl.BlockSpec((dy.shape[0], chunk), lambda i: (0, i)),
                pl.BlockSpec((rows, chunk), lambda i, at=at: (0, at + i)),
                pl.BlockSpec((chunk, K), lambda i, at=at: (at + i, 0)),
                pl.BlockSpec((rows, 1), lambda i: (0, 0)),
                pl.BlockSpec((1, K), lambda i: (0, 0)),
            ],
            out_specs=pl.BlockSpec((groups * SEQS, K), lambda i: (0, 0)),
            out_shape=jax.ShapeDtypeStruct((groups * SEQS, K), jnp.float32),
            scratch_shapes=[pltpu.VMEM((rows, K), jnp.float32)],
            compiler_params=pltpu.CompilerParams(vmem_limit_bytes=56 << 20),
            cost_estimate=pl.CostEstimate(
                flops=2 * groups * SEQS * rows * size * chunk * (K + 256),
                bytes_accessed=size * chunk * (rows * 4 + K * 2),
                transcendentals=0,
            ),
            name="map_piece",
        )(picked, dy, precond, signs, row_salted, row_lanes)

    with jax.named_scope("reduce"):
        norm_factor = 1.0 / jnp.sqrt(jnp.float32(D) * jnp.float32(FF))
        total = total.reshape(groups, SEQS, K) * norm_factor
        features = total[0]
        for e in range(1, groups):
            features = features + lax.ppermute(total[e], "groups", [(i, (i - e) % groups) for i in range(groups)])
        return lax.psum(features, ("wide", "narrow"))


def solution(mesh):
    placed = (
        P(("groups", "narrow"), "wide"),
        P(("groups", "wide"), "narrow"),
        P("wide", "narrow"),
        P("groups"),
        P(),
        P("wide"),
        P("narrow"),
    )
    return jax.shard_map(
        on_device, mesh=mesh, in_specs=placed, out_specs=P("groups", None), check_vma=False
    )
```

```python
import functools

import jax
import jax.numpy as jnp
from jax import lax
from jax.experimental import pallas as pl
from jax.experimental.pallas import tpu as pltpu
from jax.sharding import PartitionSpec as P

D = 5120
FF = 25600
K = 1024
SEQS = 2

adam_epsilon = 1e-08
MESH = pl.DeviceIdType.MESH


def scramble_start(number):
    number = number * 668265261
    number = number ^ lax.shift_right_logical(number, jnp.full_like(number, 15))
    number = number * 739982445
    return number ^ lax.shift_right_logical(number, jnp.full_like(number, 13))


def scramble(number):
    number = scramble_start(number) * 695872825
    return number ^ lax.shift_right_logical(number, jnp.full_like(number, 16))


LAST = ((695872825 << 11) + (1 << 31)) % (1 << 32) - (1 << 31)


def signs_of(salted, lanes):
    mixed = scramble_start(salted ^ lanes) * LAST
    return jnp.where(mixed < 0, jnp.float32(-1.0), jnp.float32(1.0))


def hash_into(out_ref, salted_ref, lanes_ref, step):
    def hash_rows(i, carry):
        part = pl.ds(pl.multiple_of(i * step, step), step)
        out_ref[part, :] = signs_of(salted_ref[part, :], lanes_ref[...]).astype(out_ref.dtype)
        return carry

    lax.fori_loop(0, out_ref.shape[0] // step, hash_rows, 0)


def ring_index(place, count):
    upper = lax.div(place, count // 2)
    return 2 * place + upper * (2 * (count - 1 - place) + 1 - 2 * place)


def prepare_kernel(
    sizes, dy_ref, x_ref, ids_ref, col_ref, col_lanes_ref, row_ref, row_lanes_ref, moment_ref,
    all_dy_ref, all_x_ref, all_ids_ref, signs_ref, precond_ref, row_signs_ref,
    own_sem, ring_send, ring_recv, cross_send, cross_recv, x_send, x_recv, ids_send, ids_recv,
):
    groups, wide, narrow = sizes
    cols = all_dy_ref.shape[3]
    step = pl.program_id(0)
    steps = cols // signs_ref.shape[0]
    g, w, n = lax.axis_index("groups"), lax.axis_index("wide"), lax.axis_index("narrow")
    half = lax.div(w, 2)
    place = half + lax.rem(w, 2) * (wide - 1 - 2 * half)
    right = ring_index(lax.rem(place + 1, wide), wide)
    left = ring_index(lax.rem(place + wide - 1, wide), wide)
    share = wide // narrow

    def own_copies():
        slots = pl.ds(n * share, share)
        return [
            pltpu.make_async_copy(dy_ref.at[:, pl.ds(pl.multiple_of(g * cols, 128), cols)], all_dy_ref.at[w, 0], own_sem.at[0]),
            pltpu.make_async_copy(x_ref, all_x_ref.at[slots, 0], own_sem.at[1]),
            pltpu.make_async_copy(ids_ref, all_ids_ref.at[0], own_sem.at[2]),
        ]

    def cross_copies():
        made = []
        for e in range(1, groups):
            target = lax.rem(g + e, groups)
            made.append(pltpu.make_async_remote_copy(
                src_ref=dy_ref.at[:, pl.ds(pl.multiple_of(target * cols, 128), cols)], dst_ref=all_dy_ref.at[w, e],
                send_sem=cross_send.at[e], recv_sem=cross_recv.at[e], device_id=(target, w, n), device_id_type=MESH))
        return made

    def small_copies():
        made = []
        slots = pl.ds(n * share, share)
        for e in range(groups):
            target = lax.rem(g + e, groups)
            for m in range(narrow):
                if e == 0 and m == 0:
                    continue
                made.append(pltpu.make_async_remote_copy(
                    src_ref=x_ref, dst_ref=all_x_ref.at[slots, e], send_sem=x_send.at[e, m], recv_sem=x_recv.at[e, m],
                    device_id=(target, w, lax.rem(n + m, narrow)), device_id_type=MESH))
            if e > 0:
                made.append(pltpu.make_async_remote_copy(
                    src_ref=ids_ref, dst_ref=all_ids_ref.at[e], send_sem=ids_send.at[e], recv_sem=ids_recv.at[e],
                    device_id=(target, w, n), device_id_type=MESH))
        return made

    def ring_copy(e, k):
        back = lax.rem(place + (wide - k if e % 2 == 0 else k), wide)
        origin = ring_index(back, wide)
        return pltpu.make_async_remote_copy(
            src_ref=all_dy_ref.at[origin, e], dst_ref=all_dy_ref.at[origin, e],
            send_sem=ring_send.at[e, k], recv_sem=ring_recv.at[e, k],
            device_id=(g, right if e % 2 == 0 else left, n), device_id_type=MESH)

    @pl.when(step == 0)
    def _():
        barrier = pltpu.get_barrier_semaphore()
        for to in (left, right):
            pl.semaphore_signal(barrier, inc=1, device_id=(g, to, n), device_id_type=MESH)
        for e in range(groups):
            for m in range(narrow):
                if e > 0 or m > 0:
                    pl.semaphore_signal(
                        barrier, inc=1, device_id=(lax.rem(g + e, groups), w, lax.rem(n + m, narrow)), device_id_type=MESH)
        pl.semaphore_wait(barrier, 1 + groups * narrow)
        for copy in cross_copies() + own_copies() + small_copies():
            copy.start()
        own_copies()[0].wait()

    last = steps - 1
    for t in range(wide + 1):

        @pl.when(step == (min(3 * t, steps - 1) if t < wide else steps - 1))
        def _(t=t):
            if t == 1:
                for copy in cross_copies():
                    copy.wait_recv()
            for e in range(groups):
                k = t - (e > 0)
                if 1 <= k <= wide - 1:
                    ring_copy(e, k - 1).wait_recv()
                if 0 <= k <= wide - 2:
                    ring_copy(e, k).start()

    @pl.when(step == 1)
    def _():
        hash_into(row_signs_ref, row_ref, row_lanes_ref, 32)

    hash_into(signs_ref, col_ref, col_lanes_ref, 64)

    def moment_rows(i, carry):
        rows = pl.ds(pl.multiple_of(i * 32, 32), 32)
        precond_ref[rows, :] = 1.0 / (jnp.sqrt(moment_ref[rows, :]) + adam_epsilon)
        return carry

    lax.fori_loop(0, moment_ref.shape[0] // 32, moment_rows, 0)

    @pl.when(step == last)
    def _():
        for copy in own_copies()[1:]:
            copy.wait()
        for copy in cross_copies():
            copy.wait_send()
        for copy in small_copies():
            copy.wait()
        for e in range(groups):
            for k in range(wide - 1):
                ring_copy(e, k).wait_send()


def map_kernel(x_ref, which_ref, dy_ref, precond_ref, signs_ref, rows_ref, out_ref, picked_ref):
    @pl.when(pl.program_id(0) == 0)
    def _():
        out_ref[...] = jnp.zeros_like(out_ref)
        turned = x_ref[...].T
        for s in range(picked_ref.shape[0]):
            picked_ref[s] = jnp.where(which_ref[...] == s, turned.astype(jnp.float32), 0.0).astype(jnp.bfloat16)

    for s in range(picked_ref.shape[0]):
        grad = jnp.dot(picked_ref[s], dy_ref[...], preferred_element_type=jnp.float32)
        scaled = (grad * precond_ref[...]).astype(jnp.bfloat16)
        mapped = jnp.dot(scaled, signs_ref[...], preferred_element_type=jnp.float32)
        out_ref[s : s + 1, :] += jnp.sum(mapped * rows_ref[...], axis=0, keepdims=True)


def reduce_kernel(sizes, terms_ref, out_ref, near, mine, far, near_send, near_recv, far_send, far_recv):
    groups, wide, narrow = sizes
    g, w, n = lax.axis_index("groups"), lax.axis_index("wide"), lax.axis_index("narrow")

    def near_copy(e, m):
        return pltpu.make_async_remote_copy(
            src_ref=terms_ref.at[e], dst_ref=near.at[e * narrow + m],
            send_sem=near_send.at[e * narrow + m], recv_sem=near_recv.at[e * narrow + m],
            device_id=(lax.rem(g + groups - e, groups), w, lax.rem(n + m, narrow)), device_id_type=MESH)

    def far_copy(v):
        return pltpu.make_async_remote_copy(
            src_ref=mine, dst_ref=far.at[v], send_sem=far_send.at[v], recv_sem=far_recv.at[v],
            device_id=(g, lax.rem(w + v, wide), n), device_id_type=MESH)

    near_list = [(e, m) for e in range(groups) for m in range(narrow) if e > 0 or m > 0]
    barrier = pltpu.get_barrier_semaphore()
    for e, m in near_list:
        pl.semaphore_signal(
            barrier, inc=1, device_id=(lax.rem(g + e, groups), w, lax.rem(n + m, narrow)), device_id_type=MESH)
    for v in range(1, wide):
        pl.semaphore_signal(barrier, inc=1, device_id=(g, lax.rem(w + v, wide), n), device_id_type=MESH)
    pl.semaphore_wait(barrier, len(near_list) + wide - 1)

    for e, m in near_list:
        near_copy(e, m).start()
    total = terms_ref[0]
    for e, m in near_list:
        near_copy(e, m).wait_recv()
        total = total + near[e * narrow + m]
    mine[...] = total
    for v in range(1, wide):
        far_copy(v).start()
    for v in range(1, wide):
        far_copy(v).wait_recv()
        total = total + far[v]
    out_ref[...] = total * (1.0 / (float(D) * float(FF)) ** 0.5)
    for e, m in near_list:
        near_copy(e, m).wait_send()
    for v in range(1, wide):
        far_copy(v).wait_send()


def on_device(activations, out_grads, second_moment, seq_ids, seed_word, row_keys, col_keys):
    sizes = groups, wide, narrow = tuple(lax.axis_size(name) for name in ("groups", "wide", "narrow"))
    me = lax.axis_index("groups")
    rows, all_cols = second_moment.shape
    cols = all_cols // groups
    tokens = seq_ids.shape[0]
    per = out_grads.shape[0]
    chunk = 1280 if cols % 1280 == 0 else 640
    small = 256 if cols % 256 == 0 else 128
    steps = cols // small

    seed = seed_word[0]
    lane = jnp.arange(K, dtype=jnp.int32)[None, :]
    row_salted = scramble(row_keys ^ (seed + 1))[:, None]
    my_keys = lax.dynamic_slice_in_dim(col_keys, me * cols, cols)
    col_salted = scramble(my_keys ^ (seed + 2))[:, None]
    row_lanes = scramble(lane + 1)
    col_lanes = scramble(lane + 2)

    any_space = pl.BlockSpec(memory_space=pl.ANY)
    dma = pltpu.SemaphoreType.DMA
    all_dy, all_x, all_ids, signs, precond, row_signs = pl.pallas_call(
        functools.partial(prepare_kernel, sizes),
        grid=(steps,),
        in_specs=[
            any_space,
            any_space,
            any_space,
            pl.BlockSpec((small, 1), lambda i: (i, 0)),
            pl.BlockSpec((1, K), lambda i: (0, 0)),
            pl.BlockSpec((rows, 1), lambda i: (0, 0)),
            pl.BlockSpec((1, K), lambda i: (0, 0)),
            pl.BlockSpec((rows, small), lambda i: (0, lax.axis_index("groups") * steps + i)),
        ],
        out_specs=[
            any_space,
            any_space,
            any_space,
            pl.BlockSpec((small, K), lambda i: (i, 0)),
            pl.BlockSpec((rows, small), lambda i: (0, i)),
            pl.BlockSpec((rows, K), lambda i: (0, 0)),
        ],
        out_shape=[
            jax.ShapeDtypeStruct((wide, groups, per, cols), jnp.bfloat16),
            jax.ShapeDtypeStruct((wide, groups, per, rows), jnp.bfloat16),
            jax.ShapeDtypeStruct((groups, 1, tokens), jnp.int32),
            jax.ShapeDtypeStruct((cols, K), jnp.bfloat16),
            jax.ShapeDtypeStruct((rows, cols), jnp.float32),
            jax.ShapeDtypeStruct((rows, K), jnp.float32),
        ],
        scratch_shapes=[
            dma((3,)),
            dma((groups, wide)),
            dma((groups, wide)),
            dma((groups,)),
            dma((groups,)),
            dma((groups, narrow)),
            dma((groups, narrow)),
            dma((groups,)),
            dma((groups,)),
        ],
        compiler_params=pltpu.CompilerParams(vmem_limit_bytes=40 << 20, collective_id=0, has_side_effects=True),
        cost_estimate=pl.CostEstimate(flops=cols * K * 20, bytes_accessed=rows * cols * 8 + cols * K * 2, transcendentals=2 * rows * cols),
        name="prepare",
    )(
        out_grads, activations.reshape(wide // narrow, per, rows), seq_ids.reshape(1, tokens),
        col_salted, col_lanes, row_salted, row_lanes, second_moment,
    )

    count = groups * tokens
    which = all_ids.reshape(groups, wide, per) + SEQS * jnp.arange(groups, dtype=jnp.int32)[:, None, None]
    which = which.transpose(1, 0, 2).reshape(1, count)

    terms = pl.pallas_call(
        map_kernel,
        grid=(cols // chunk,),
        in_specs=[
            pl.BlockSpec((count, rows), lambda i: (0, 0)),
            pl.BlockSpec((1, count), lambda i: (0, 0)),
            pl.BlockSpec((count, chunk), lambda i: (0, i)),
            pl.BlockSpec((rows, chunk), lambda i: (0, i)),
            pl.BlockSpec((chunk, K), lambda i: (i, 0)),
            pl.BlockSpec((rows, K), lambda i: (0, 0)),
        ],
        out_specs=pl.BlockSpec((groups * SEQS, K), lambda i: (0, 0)),
        out_shape=jax.ShapeDtypeStruct((groups * SEQS, K), jnp.float32),
        scratch_shapes=[pltpu.VMEM((groups * SEQS, rows, count), jnp.bfloat16)],
        compiler_params=pltpu.CompilerParams(vmem_limit_bytes=58 << 20),
        cost_estimate=pl.CostEstimate(
            flops=2 * groups * SEQS * rows * cols * (K + 256), bytes_accessed=cols * (rows * 4 + K * 2), transcendentals=0),
        name="map",
    )(all_x.reshape(count, rows), which, all_dy.reshape(count, cols), precond, signs, row_signs)

    close = groups * narrow
    return pl.pallas_call(
        functools.partial(reduce_kernel, sizes),
        in_specs=[pl.BlockSpec(memory_space=pltpu.VMEM)],
        out_specs=pl.BlockSpec(memory_space=pltpu.VMEM),
        out_shape=jax.ShapeDtypeStruct((SEQS, K), jnp.float32),
        scratch_shapes=[
            pltpu.VMEM((close, SEQS, K), jnp.float32),
            pltpu.VMEM((SEQS, K), jnp.float32),
            pltpu.VMEM((wide, SEQS, K), jnp.float32),
            dma((close,)),
            dma((close,)),
            dma((wide,)),
            dma((wide,)),
        ],
        compiler_params=pltpu.CompilerParams(collective_id=1, has_side_effects=True),
        name="reduce",
    )(terms.reshape(groups, SEQS, K))


def solution(mesh):
    placed = (
        P(("groups", "narrow"), "wide"),
        P(("groups", "wide"), "narrow"),
        P("wide", "narrow"),
        P("groups"),
        P(),
        P("wide"),
        P("narrow"),
    )
    return jax.shard_map(
        on_device, mesh=mesh, in_specs=placed, out_specs=P("groups", None), check_vma=False
    )
```

```python
import functools

import jax
import jax.numpy as jnp
from jax import lax
from jax.experimental import pallas as pl
from jax.experimental.pallas import tpu as pltpu
from jax.sharding import PartitionSpec as P

D = 5120
FF = 25600
K = 1024
SEQS = 2

adam_epsilon = 1e-08
MESH = pl.DeviceIdType.MESH


def scramble_start(number):
    number = number * 668265261
    number = number ^ lax.shift_right_logical(number, jnp.full_like(number, 15))
    number = number * 739982445
    return number ^ lax.shift_right_logical(number, jnp.full_like(number, 13))


def scramble(number):
    number = scramble_start(number) * 695872825
    return number ^ lax.shift_right_logical(number, jnp.full_like(number, 16))


LAST = ((695872825 << 11) + (1 << 31)) % (1 << 32) - (1 << 31)


def signs_of(salted, lanes):
    mixed = scramble_start(salted ^ lanes) * LAST
    return jnp.where(mixed < 0, jnp.float32(-1.0), jnp.float32(1.0))


def hash_into(out_ref, salted_ref, lanes_ref, step):
    def hash_rows(i, carry):
        part = pl.ds(pl.multiple_of(i * step, step), step)
        out_ref[part, :] = signs_of(salted_ref[part, :], lanes_ref[...]).astype(out_ref.dtype)
        return carry

    lax.fori_loop(0, out_ref.shape[0] // step, hash_rows, 0)


def ring_index(place, count):
    upper = lax.div(place, count // 2)
    return 2 * place + upper * (2 * (count - 1 - place) + 1 - 2 * place)


class Ring:
    def __init__(self, sizes, dy_ref, into_ref, sems, base, cols):
        self.sizes, self.dy_ref, self.into_ref = sizes, dy_ref, into_ref
        self.own_sem, self.send, self.recv, self.cross_send, self.cross_recv = sems
        self.base, self.cols, self.width = base, cols, into_ref.shape[3]
        wide = sizes[1]
        self.g, self.w, self.n = lax.axis_index("groups"), lax.axis_index("wide"), lax.axis_index("narrow")
        half = lax.div(self.w, 2)
        self.place = half + lax.rem(self.w, 2) * (wide - 1 - 2 * half)
        self.right = ring_index(lax.rem(self.place + 1, wide), wide)
        self.left = ring_index(lax.rem(self.place + wide - 1, wide), wide)

    def block(self, group):
        start = pl.multiple_of(group * self.cols + self.base, 128)
        return self.dy_ref.at[:, pl.ds(start, self.width)]

    def own(self):
        return pltpu.make_async_copy(self.block(self.g), self.into_ref.at[self.w, 0], self.own_sem.at[0])

    def cross(self):
        made = []
        for e in range(1, self.sizes[0]):
            target = lax.rem(self.g + e, self.sizes[0])
            made.append(pltpu.make_async_remote_copy(
                src_ref=self.block(target), dst_ref=self.into_ref.at[self.w, e],
                send_sem=self.cross_send.at[e], recv_sem=self.cross_recv.at[e],
                device_id=(target, self.w, self.n), device_id_type=MESH))
        return made

    def hop(self, e, k):
        wide = self.sizes[1]
        origin = ring_index(lax.rem(self.place + (wide - k if e % 2 == 0 else k), wide), wide)
        return pltpu.make_async_remote_copy(
            src_ref=self.into_ref.at[origin, e], dst_ref=self.into_ref.at[origin, e],
            send_sem=self.send.at[e, k], recv_sem=self.recv.at[e, k],
            device_id=(self.g, self.right if e % 2 == 0 else self.left, self.n), device_id_type=MESH)

    def stage(self, t):
        groups, wide, _ = self.sizes
        if t == 0:
            for copy in self.cross() + [self.own()]:
                copy.start()
            self.own().wait()
        if t == 1:
            for copy in self.cross():
                copy.wait_recv()
        for e in range(groups):
            k = t - (e > 0)
            if 1 <= k <= wide - 1:
                self.hop(e, k - 1).wait_recv()
            if 0 <= k <= wide - 2:
                self.hop(e, k).start()

    def finish(self):
        for copy in self.cross():
            copy.wait_send()
        for e in range(self.sizes[0]):
            for k in range(self.sizes[1] - 1):
                self.hop(e, k).wait_send()


def ring_semaphores(sizes):
    dma = pltpu.SemaphoreType.DMA
    return [dma((1,)), dma(sizes[:2]), dma(sizes[:2]), dma(sizes[:1]), dma(sizes[:1])]


def greet(sizes, left, right, cores):
    groups, _, narrow = sizes
    g, w, n = lax.axis_index("groups"), lax.axis_index("wide"), lax.axis_index("narrow")
    barrier = pltpu.get_barrier_semaphore()
    for to in (left, right):
        pl.semaphore_signal(barrier, inc=1, device_id=(g, to, n), device_id_type=MESH)
    for e in range(groups):
        for m in range(cores):
            if e > 0 or m > 0:
                pl.semaphore_signal(
                    barrier, inc=1, device_id=(lax.rem(g + e, groups), w, lax.rem(n + m, narrow)), device_id_type=MESH)
    pl.semaphore_wait(barrier, 1 + groups * cores)


def prepare_kernel(
    sizes, cols, dy_ref, x_ref, ids_ref, col_ref, col_lanes_ref, row_ref, row_lanes_ref, moment_ref,
    all_dy_ref, all_x_ref, all_ids_ref, signs_ref, precond_ref, row_signs_ref,
    small_sem, x_send, x_recv, ids_send, ids_recv, *ring_sems,
):
    groups, wide, narrow = sizes
    step = pl.program_id(0)
    steps = cols // signs_ref.shape[0]
    g, w, n = lax.axis_index("groups"), lax.axis_index("wide"), lax.axis_index("narrow")
    share = wide // narrow
    ring = Ring(sizes, dy_ref, all_dy_ref, ring_sems, 0, cols)

    def own_copies():
        return [
            pltpu.make_async_copy(x_ref, all_x_ref.at[pl.ds(n * share, share), 0], small_sem.at[0]),
            pltpu.make_async_copy(ids_ref, all_ids_ref.at[0], small_sem.at[1]),
        ]

    def small_copies():
        made = []
        slots = pl.ds(n * share, share)
        for e in range(groups):
            target = lax.rem(g + e, groups)
            for m in range(narrow):
                if e == 0 and m == 0:
                    continue
                made.append(pltpu.make_async_remote_copy(
                    src_ref=x_ref, dst_ref=all_x_ref.at[slots, e], send_sem=x_send.at[e, m], recv_sem=x_recv.at[e, m],
                    device_id=(target, w, lax.rem(n + m, narrow)), device_id_type=MESH))
            if e > 0:
                made.append(pltpu.make_async_remote_copy(
                    src_ref=ids_ref, dst_ref=all_ids_ref.at[e], send_sem=ids_send.at[e], recv_sem=ids_recv.at[e],
                    device_id=(target, w, n), device_id_type=MESH))
        return made

    @pl.when(step == 0)
    def _():
        greet(sizes, ring.left, ring.right, narrow)

    last = steps - 1
    for t in range(wide + 1):

        @pl.when(step == (min(3 * t, last) if t < wide else last))
        def _(t=t):
            ring.stage(t)

    @pl.when(step == 0)
    def _():
        for copy in own_copies() + small_copies():
            copy.start()

    @pl.when(step == 1)
    def _():
        hash_into(row_signs_ref, row_ref, row_lanes_ref, 32)

    hash_into(signs_ref, col_ref, col_lanes_ref, 64)

    def moment_rows(i, carry):
        rows = pl.ds(pl.multiple_of(i * 32, 32), 32)
        precond_ref[rows, :] = 1.0 / (jnp.sqrt(moment_ref[rows, :]) + adam_epsilon)
        return carry

    lax.fori_loop(0, moment_ref.shape[0] // 32, moment_rows, 0)

    @pl.when(step == last)
    def _():
        for copy in own_copies() + small_copies():
            copy.wait()
        ring.finish()


def map_kernel(
    sizes, cols, early, x_ref, which_ref, early_dy_ref, dy_ref, precond_ref, signs_ref, rows_ref,
    out_ref, picked_ref, late_ref, now_ref, *ring_sems,
):
    groups, wide, _ = sizes
    i = pl.program_id(0)
    count, chunk = now_ref.shape
    many = picked_ref.shape[0]
    chunks = cols // chunk
    ring = Ring(sizes, dy_ref, late_ref, ring_sems, early * chunk, cols)
    stages = wide + 1
    slots = early * many

    @pl.when(i == 0)
    def _():
        greet(sizes, ring.left, ring.right, 1)
        ring.stage(0)
        out_ref[...] = jnp.zeros_like(out_ref)
        turned = x_ref[...].T.astype(jnp.float32)
        for s in range(many):
            picked_ref[s] = jnp.where(which_ref[...] == s, turned, 0.0).astype(jnp.bfloat16)

    @pl.when(i < early)
    def _():
        now_ref[...] = early_dy_ref[...]

    for c in range(early, chunks):

        @pl.when(i == c)
        def _(c=c):
            now_ref[...] = late_ref[:, :, :, (c - early) * chunk : (c - early + 1) * chunk].reshape(count, chunk)

    for s in range(many):
        for t in range(1, stages):
            slot = t if stages <= slots else t * slots // stages
            if slot % many == s:

                @pl.when(i == slot // many)
                def _(t=t):
                    ring.stage(t)

        grad = jnp.dot(picked_ref[s], now_ref[...], preferred_element_type=jnp.float32)
        scaled = (grad * precond_ref[...]).astype(jnp.bfloat16)
        mapped = jnp.dot(scaled, signs_ref[...], preferred_element_type=jnp.float32)
        out_ref[s // SEQS, s % SEQS : s % SEQS + 1, :] += jnp.sum(mapped * rows_ref[...], axis=0, keepdims=True)

    @pl.when(i == chunks - 1)
    def _():
        ring.finish()


def reduce_kernel(sizes, terms_ref, out_ref, near, mine, far, near_send, near_recv, far_send, far_recv):
    groups, wide, narrow = sizes
    g, w, n = lax.axis_index("groups"), lax.axis_index("wide"), lax.axis_index("narrow")

    def near_copy(e, m):
        return pltpu.make_async_remote_copy(
            src_ref=terms_ref.at[e], dst_ref=near.at[e * narrow + m],
            send_sem=near_send.at[e * narrow + m], recv_sem=near_recv.at[e * narrow + m],
            device_id=(lax.rem(g + groups - e, groups), w, lax.rem(n + m, narrow)), device_id_type=MESH)

    def far_copy(v):
        return pltpu.make_async_remote_copy(
            src_ref=mine, dst_ref=far.at[v], send_sem=far_send.at[v], recv_sem=far_recv.at[v],
            device_id=(g, lax.rem(w + v, wide), n), device_id_type=MESH)

    near_list = [(e, m) for e in range(groups) for m in range(narrow) if e > 0 or m > 0]
    barrier = pltpu.get_barrier_semaphore()
    for e, m in near_list:
        pl.semaphore_signal(
            barrier, inc=1, device_id=(lax.rem(g + e, groups), w, lax.rem(n + m, narrow)), device_id_type=MESH)
    for v in range(1, wide):
        pl.semaphore_signal(barrier, inc=1, device_id=(g, lax.rem(w + v, wide), n), device_id_type=MESH)
    pl.semaphore_wait(barrier, len(near_list) + wide - 1)

    for e, m in near_list:
        near_copy(e, m).start()
    total = terms_ref[0]
    for e, m in near_list:
        near_copy(e, m).wait_recv()
        total = total + near[e * narrow + m]
    mine[...] = total
    for v in range(1, wide):
        far_copy(v).start()
    for v in range(1, wide):
        far_copy(v).wait_recv()
        total = total + far[v]
    out_ref[...] = total * (1.0 / (float(D) * float(FF)) ** 0.5)
    for e, m in near_list:
        near_copy(e, m).wait_send()
    for v in range(1, wide):
        far_copy(v).wait_send()


def on_device(activations, out_grads, second_moment, seq_ids, seed_word, row_keys, col_keys):
    sizes = groups, wide, narrow = tuple(lax.axis_size(name) for name in ("groups", "wide", "narrow"))
    me = lax.axis_index("groups")
    rows, all_cols = second_moment.shape
    cols = all_cols // groups
    tokens = seq_ids.shape[0]
    per = out_grads.shape[0]
    chunk = 1280 if cols % 1280 == 0 else 640
    small = 256 if cols % 256 == 0 else 128
    steps = cols // small
    chunks = cols // chunk
    early = chunks - 2

    seed = seed_word[0]
    lane = jnp.arange(K, dtype=jnp.int32)[None, :]
    row_salted = scramble(row_keys ^ (seed + 1))[:, None]
    my_keys = lax.dynamic_slice_in_dim(col_keys, me * cols, cols)
    col_salted = scramble(my_keys ^ (seed + 2))[:, None]
    row_lanes = scramble(lane + 1)
    col_lanes = scramble(lane + 2)

    any_space = pl.BlockSpec(memory_space=pl.ANY)
    dma = pltpu.SemaphoreType.DMA
    all_dy, all_x, all_ids, signs, precond, row_signs = pl.pallas_call(
        functools.partial(prepare_kernel, sizes, cols),
        grid=(steps,),
        in_specs=[
            any_space,
            any_space,
            any_space,
            pl.BlockSpec((small, 1), lambda i: (i, 0)),
            pl.BlockSpec((1, K), lambda i: (0, 0)),
            pl.BlockSpec((rows, 1), lambda i: (0, 0)),
            pl.BlockSpec((1, K), lambda i: (0, 0)),
            pl.BlockSpec((rows, small), lambda i: (0, lax.axis_index("groups") * steps + i)),
        ],
        out_specs=[
            any_space,
            any_space,
            any_space,
            pl.BlockSpec((small, K), lambda i: (i, 0)),
            pl.BlockSpec((rows, small), lambda i: (0, i)),
            pl.BlockSpec((rows, K), lambda i: (0, 0)),
        ],
        out_shape=[
            jax.ShapeDtypeStruct((wide, groups, per, early * chunk), jnp.bfloat16),
            jax.ShapeDtypeStruct((wide, groups, per, rows), jnp.bfloat16),
            jax.ShapeDtypeStruct((groups, 1, tokens), jnp.int32),
            jax.ShapeDtypeStruct((cols, K), jnp.bfloat16),
            jax.ShapeDtypeStruct((rows, cols), jnp.float32),
            jax.ShapeDtypeStruct((rows, K), jnp.float32),
        ],
        scratch_shapes=[
            dma((2,)), dma((groups, narrow)), dma((groups, narrow)), dma((groups,)), dma((groups,)),
            *ring_semaphores(sizes),
        ],
        compiler_params=pltpu.CompilerParams(vmem_limit_bytes=60 << 20, collective_id=0, has_side_effects=True),
        cost_estimate=pl.CostEstimate(flops=cols * K * 20, bytes_accessed=rows * cols * 8 + cols * K * 2, transcendentals=2 * rows * cols),
        name="prepare",
    )(
        out_grads, activations.reshape(wide // narrow, per, rows), seq_ids.reshape(1, tokens),
        col_salted, col_lanes, row_salted, row_lanes, second_moment,
    )

    count = groups * tokens
    which = all_ids.reshape(groups, wide, per) + SEQS * jnp.arange(groups, dtype=jnp.int32)[:, None, None]
    which = which.transpose(1, 0, 2).reshape(1, count)

    terms = pl.pallas_call(
        functools.partial(map_kernel, sizes, cols, early),
        grid=(cols // chunk,),
        in_specs=[
            pl.BlockSpec((count, rows), lambda i: (0, 0)),
            pl.BlockSpec((1, count), lambda i: (0, 0)),
            pl.BlockSpec((count, chunk), lambda i: (0, jnp.minimum(i, early - 1))),
            any_space,
            pl.BlockSpec((rows, chunk), lambda i: (0, i)),
            pl.BlockSpec((chunk, K), lambda i: (i, 0)),
            pl.BlockSpec((rows, K), lambda i: (0, 0)),
        ],
        out_specs=pl.BlockSpec((groups, SEQS, K), lambda i: (0, 0, 0)),
        out_shape=jax.ShapeDtypeStruct((groups, SEQS, K), jnp.float32),
        scratch_shapes=[
            pltpu.VMEM((groups * SEQS, rows, count), jnp.bfloat16),
            pltpu.VMEM((wide, groups, per, (chunks - early) * chunk), jnp.bfloat16),
            pltpu.VMEM((count, chunk), jnp.bfloat16),
            *ring_semaphores(sizes),
        ],
        compiler_params=pltpu.CompilerParams(vmem_limit_bytes=60 << 20, collective_id=2, has_side_effects=True),
        cost_estimate=pl.CostEstimate(
            flops=2 * groups * SEQS * rows * cols * (K + 256), bytes_accessed=cols * (rows * 4 + K * 2), transcendentals=0),
        name="map",
    )(all_x.reshape(count, rows), which, all_dy.reshape(count, early * chunk), out_grads, precond, signs, row_signs)

    close = groups * narrow
    return pl.pallas_call(
        functools.partial(reduce_kernel, sizes),
        in_specs=[pl.BlockSpec(memory_space=pltpu.VMEM)],
        out_specs=pl.BlockSpec(memory_space=pltpu.VMEM),
        out_shape=jax.ShapeDtypeStruct((SEQS, K), jnp.float32),
        scratch_shapes=[
            pltpu.VMEM((close, SEQS, K), jnp.float32),
            pltpu.VMEM((SEQS, K), jnp.float32),
            pltpu.VMEM((wide, SEQS, K), jnp.float32),
            dma((close,)),
            dma((close,)),
            dma((wide,)),
            dma((wide,)),
        ],
        compiler_params=pltpu.CompilerParams(collective_id=1, has_side_effects=True),
        name="reduce",
    )(terms)


def solution(mesh):
    placed = (
        P(("groups", "narrow"), "wide"),
        P(("groups", "wide"), "narrow"),
        P("wide", "narrow"),
        P("groups"),
        P(),
        P("wide"),
        P("narrow"),
    )
    return jax.shard_map(
        on_device, mesh=mesh, in_specs=placed, out_specs=P("groups", None), check_vma=False
    )
```

```python
import functools

import jax
import jax.numpy as jnp
from jax import lax
from jax.experimental import pallas as pl
from jax.experimental.pallas import tpu as pltpu
from jax.sharding import PartitionSpec as P

D = 5120
FF = 25600
K = 1024
SEQS = 2

adam_epsilon = 1e-08
MESH = pl.DeviceIdType.MESH


def scramble_start(number):
    number = number * 668265261
    number = number ^ lax.shift_right_logical(number, jnp.full_like(number, 15))
    number = number * 739982445
    return number ^ lax.shift_right_logical(number, jnp.full_like(number, 13))


def scramble(number):
    number = scramble_start(number) * 695872825
    return number ^ lax.shift_right_logical(number, jnp.full_like(number, 16))


LAST = ((695872825 << 11) + (1 << 31)) % (1 << 32) - (1 << 31)


def signs_of(salted, lanes):
    mixed = scramble_start(salted ^ lanes) * LAST
    return jnp.where(mixed < 0, jnp.float32(-1.0), jnp.float32(1.0))


def hash_into(out_ref, salted_ref, lanes_ref, step):
    def hash_rows(i, carry):
        part = pl.ds(pl.multiple_of(i * step, step), step)
        out_ref[part, :] = signs_of(salted_ref[part, :], lanes_ref[...]).astype(out_ref.dtype)
        return carry

    lax.fori_loop(0, out_ref.shape[0] // step, hash_rows, 0)


def ring_index(place, count):
    upper = lax.div(place, count // 2)
    return 2 * place + upper * (2 * (count - 1 - place) + 1 - 2 * place)


def prepare_kernel(
    sizes, dy_ref, x_ref, ids_ref, col_ref, col_lanes_ref, row_ref, row_lanes_ref, moment_ref,
    all_dy_ref, all_x_ref, all_ids_ref, signs_ref, precond_ref, row_signs_ref,
    own_sem, ring_send, ring_recv, cross_send, cross_recv, x_send, x_recv, ids_send, ids_recv,
):
    groups, wide, narrow = sizes
    cols = all_dy_ref.shape[3]
    step = pl.program_id(0)
    steps = cols // signs_ref.shape[0]
    g, w, n = lax.axis_index("groups"), lax.axis_index("wide"), lax.axis_index("narrow")
    half = lax.div(w, 2)
    place = half + lax.rem(w, 2) * (wide - 1 - 2 * half)
    right = ring_index(lax.rem(place + 1, wide), wide)
    left = ring_index(lax.rem(place + wide - 1, wide), wide)
    share = wide // narrow

    def own_copies():
        slots = pl.ds(n * share, share)
        return [
            pltpu.make_async_copy(dy_ref.at[:, pl.ds(pl.multiple_of(g * cols, 128), cols)], all_dy_ref.at[w, 0], own_sem.at[0]),
            pltpu.make_async_copy(x_ref, all_x_ref.at[slots, 0], own_sem.at[1]),
            pltpu.make_async_copy(ids_ref, all_ids_ref.at[0], own_sem.at[2]),
        ]

    def cross_copies():
        made = []
        for e in range(1, groups):
            target = lax.rem(g + e, groups)
            made.append(pltpu.make_async_remote_copy(
                src_ref=dy_ref.at[:, pl.ds(pl.multiple_of(target * cols, 128), cols)], dst_ref=all_dy_ref.at[w, e],
                send_sem=cross_send.at[e], recv_sem=cross_recv.at[e], device_id=(target, w, n), device_id_type=MESH))
        return made

    def small_copies():
        made = []
        slots = pl.ds(n * share, share)
        for e in range(groups):
            target = lax.rem(g + e, groups)
            for m in range(narrow):
                if e == 0 and m == 0:
                    continue
                made.append(pltpu.make_async_remote_copy(
                    src_ref=x_ref, dst_ref=all_x_ref.at[slots, e], send_sem=x_send.at[e, m], recv_sem=x_recv.at[e, m],
                    device_id=(target, w, lax.rem(n + m, narrow)), device_id_type=MESH))
            if e > 0:
                made.append(pltpu.make_async_remote_copy(
                    src_ref=ids_ref, dst_ref=all_ids_ref.at[e], send_sem=ids_send.at[e], recv_sem=ids_recv.at[e],
                    device_id=(target, w, n), device_id_type=MESH))
        return made

    def ring_copy(e, k):
        back = lax.rem(place + (wide - k if e % 2 == 0 else k), wide)
        origin = ring_index(back, wide)
        return pltpu.make_async_remote_copy(
            src_ref=all_dy_ref.at[origin, e], dst_ref=all_dy_ref.at[origin, e],
            send_sem=ring_send.at[e, k], recv_sem=ring_recv.at[e, k],
            device_id=(g, right if e % 2 == 0 else left, n), device_id_type=MESH)

    @pl.when(step == 0)
    def _():
        barrier = pltpu.get_barrier_semaphore()
        for to in (left, right):
            pl.semaphore_signal(barrier, inc=1, device_id=(g, to, n), device_id_type=MESH)
        for e in range(groups):
            for m in range(narrow):
                if e > 0 or m > 0:
                    pl.semaphore_signal(
                        barrier, inc=1, device_id=(lax.rem(g + e, groups), w, lax.rem(n + m, narrow)), device_id_type=MESH)
        pl.semaphore_wait(barrier, 1 + groups * narrow)
        for copy in cross_copies() + own_copies() + small_copies():
            copy.start()
        own_copies()[0].wait()

    last = steps - 1
    for t in range(wide + 1):

        @pl.when(step == (min(3 * t, steps - 1) if t < wide else steps - 1))
        def _(t=t):
            if t == 1:
                for copy in cross_copies():
                    copy.wait_recv()
            for e in range(groups):
                k = t - (e > 0)
                if 1 <= k <= wide - 1:
                    ring_copy(e, k - 1).wait_recv()
                if 0 <= k <= wide - 2:
                    ring_copy(e, k).start()

    @pl.when(step == 1)
    def _():
        hash_into(row_signs_ref, row_ref, row_lanes_ref, 32)

    turns = signs_ref.shape[0] // 64
    share_rows = moment_ref.shape[0] // turns

    def turn(i, carry):
        part = pl.ds(pl.multiple_of(i * 64, 64), 64)
        rows = pl.ds(pl.multiple_of(i * share_rows, 16), share_rows)
        precond_ref[rows, :] = 1.0 / (jnp.sqrt(moment_ref[rows, :]) + adam_epsilon)
        signs_ref[part, :] = signs_of(col_ref[part, :], col_lanes_ref[...]).astype(jnp.bfloat16)
        return carry

    lax.fori_loop(0, turns, turn, 0)

    @pl.when(step == last)
    def _():
        for copy in own_copies()[1:]:
            copy.wait()
        for copy in cross_copies():
            copy.wait_send()
        for copy in small_copies():
            copy.wait()
        for e in range(groups):
            for k in range(wide - 1):
                ring_copy(e, k).wait_send()


def map_kernel(x_ref, which_ref, dy_ref, precond_ref, signs_ref, rows_ref, out_ref, picked_ref):
    @pl.when(pl.program_id(0) == 0)
    def _():
        out_ref[...] = jnp.zeros_like(out_ref)
        turned = x_ref[...].T
        for s in range(picked_ref.shape[0]):
            picked_ref[s] = jnp.where(which_ref[...] == s, turned.astype(jnp.float32), 0.0).astype(jnp.bfloat16)

    for s in range(picked_ref.shape[0]):
        grad = jnp.dot(picked_ref[s], dy_ref[...], preferred_element_type=jnp.float32)
        scaled = (grad * precond_ref[...]).astype(jnp.bfloat16)
        mapped = jnp.dot(scaled, signs_ref[...], preferred_element_type=jnp.float32)
        out_ref[s // SEQS, s % SEQS : s % SEQS + 1, :] += jnp.sum(mapped * rows_ref[...], axis=0, keepdims=True)


def reduce_kernel(sizes, terms_ref, out_ref, near, mine, far, near_send, near_recv, far_send, far_recv):
    groups, wide, narrow = sizes
    g, w, n = lax.axis_index("groups"), lax.axis_index("wide"), lax.axis_index("narrow")

    def near_copy(e, m):
        return pltpu.make_async_remote_copy(
            src_ref=terms_ref.at[e], dst_ref=near.at[e * narrow + m],
            send_sem=near_send.at[e * narrow + m], recv_sem=near_recv.at[e * narrow + m],
            device_id=(lax.rem(g + groups - e, groups), w, lax.rem(n + m, narrow)), device_id_type=MESH)

    def far_copy(v):
        return pltpu.make_async_remote_copy(
            src_ref=mine, dst_ref=far.at[v], send_sem=far_send.at[v], recv_sem=far_recv.at[v],
            device_id=(g, lax.rem(w + v, wide), n), device_id_type=MESH)

    near_list = [(e, m) for e in range(groups) for m in range(narrow) if e > 0 or m > 0]
    barrier = pltpu.get_barrier_semaphore()
    for e, m in near_list:
        pl.semaphore_signal(
            barrier, inc=1, device_id=(lax.rem(g + e, groups), w, lax.rem(n + m, narrow)), device_id_type=MESH)
    for v in range(1, wide):
        pl.semaphore_signal(barrier, inc=1, device_id=(g, lax.rem(w + v, wide), n), device_id_type=MESH)
    pl.semaphore_wait(barrier, len(near_list) + wide - 1)

    for e, m in near_list:
        near_copy(e, m).start()
    total = terms_ref[0]
    for e, m in near_list:
        near_copy(e, m).wait_recv()
        total = total + near[e * narrow + m]
    mine[...] = total
    for v in range(1, wide):
        far_copy(v).start()
    for v in range(1, wide):
        far_copy(v).wait_recv()
        total = total + far[v]
    out_ref[...] = total * (1.0 / (float(D) * float(FF)) ** 0.5)
    for e, m in near_list:
        near_copy(e, m).wait_send()
    for v in range(1, wide):
        far_copy(v).wait_send()


def on_device(activations, out_grads, second_moment, seq_ids, seed_word, row_keys, col_keys):
    sizes = groups, wide, narrow = tuple(lax.axis_size(name) for name in ("groups", "wide", "narrow"))
    me = lax.axis_index("groups")
    rows, all_cols = second_moment.shape
    cols = all_cols // groups
    tokens = seq_ids.shape[0]
    per = out_grads.shape[0]
    chunk = 1280 if cols % 1280 == 0 else 640
    small = 256 if cols % 256 == 0 else 128
    steps = cols // small

    seed = seed_word[0]
    lane = jnp.arange(K, dtype=jnp.int32)[None, :]
    row_salted = scramble(row_keys ^ (seed + 1))[:, None]
    my_keys = lax.dynamic_slice_in_dim(col_keys, me * cols, cols)
    col_salted = scramble(my_keys ^ (seed + 2))[:, None]
    row_lanes = scramble(lane + 1)
    col_lanes = scramble(lane + 2)

    any_space = pl.BlockSpec(memory_space=pl.ANY)
    dma = pltpu.SemaphoreType.DMA
    all_dy, all_x, all_ids, signs, precond, row_signs = pl.pallas_call(
        functools.partial(prepare_kernel, sizes),
        grid=(steps,),
        in_specs=[
            any_space,
            any_space,
            any_space,
            pl.BlockSpec((small, 1), lambda i: (i, 0)),
            pl.BlockSpec((1, K), lambda i: (0, 0)),
            pl.BlockSpec((rows, 1), lambda i: (0, 0)),
            pl.BlockSpec((1, K), lambda i: (0, 0)),
            pl.BlockSpec((rows, small), lambda i: (0, lax.axis_index("groups") * steps + i)),
        ],
        out_specs=[
            any_space,
            any_space,
            any_space,
            pl.BlockSpec((small, K), lambda i: (i, 0)),
            pl.BlockSpec((rows, small), lambda i: (0, i)),
            pl.BlockSpec((rows, K), lambda i: (0, 0)),
        ],
        out_shape=[
            jax.ShapeDtypeStruct((wide, groups, per, cols), jnp.bfloat16),
            jax.ShapeDtypeStruct((wide, groups, per, rows), jnp.bfloat16),
            jax.ShapeDtypeStruct((groups, 1, tokens), jnp.int32),
            jax.ShapeDtypeStruct((cols, K), jnp.bfloat16),
            jax.ShapeDtypeStruct((rows, cols), jnp.float32),
            jax.ShapeDtypeStruct((rows, K), jnp.float32),
        ],
        scratch_shapes=[
            dma((3,)),
            dma((groups, wide)),
            dma((groups, wide)),
            dma((groups,)),
            dma((groups,)),
            dma((groups, narrow)),
            dma((groups, narrow)),
            dma((groups,)),
            dma((groups,)),
        ],
        compiler_params=pltpu.CompilerParams(vmem_limit_bytes=40 << 20, collective_id=0, has_side_effects=True),
        cost_estimate=pl.CostEstimate(flops=cols * K * 20, bytes_accessed=rows * cols * 8 + cols * K * 2, transcendentals=2 * rows * cols),
        name="prepare",
    )(
        out_grads, activations.reshape(wide // narrow, per, rows), seq_ids.reshape(1, tokens),
        col_salted, col_lanes, row_salted, row_lanes, second_moment,
    )

    count = groups * tokens
    which = all_ids.reshape(groups, wide, per) + SEQS * jnp.arange(groups, dtype=jnp.int32)[:, None, None]
    which = which.transpose(1, 0, 2).reshape(1, count)

    terms = pl.pallas_call(
        map_kernel,
        grid=(cols // chunk,),
        in_specs=[
            pl.BlockSpec((count, rows), lambda i: (0, 0)),
            pl.BlockSpec((1, count), lambda i: (0, 0)),
            pl.BlockSpec((count, chunk), lambda i: (0, i)),
            pl.BlockSpec((rows, chunk), lambda i: (0, i)),
            pl.BlockSpec((chunk, K), lambda i: (i, 0)),
            pl.BlockSpec((rows, K), lambda i: (0, 0)),
        ],
        out_specs=pl.BlockSpec((groups, SEQS, K), lambda i: (0, 0, 0)),
        out_shape=jax.ShapeDtypeStruct((groups, SEQS, K), jnp.float32),
        scratch_shapes=[pltpu.VMEM((groups * SEQS, rows, count), jnp.bfloat16)],
        compiler_params=pltpu.CompilerParams(vmem_limit_bytes=58 << 20),
        cost_estimate=pl.CostEstimate(
            flops=2 * groups * SEQS * rows * cols * (K + 256), bytes_accessed=cols * (rows * 4 + K * 2), transcendentals=0),
        name="map",
    )(all_x.reshape(count, rows), which, all_dy.reshape(count, cols), precond, signs, row_signs)

    close = groups * narrow
    return pl.pallas_call(
        functools.partial(reduce_kernel, sizes),
        in_specs=[pl.BlockSpec(memory_space=pltpu.VMEM)],
        out_specs=pl.BlockSpec(memory_space=pltpu.VMEM),
        out_shape=jax.ShapeDtypeStruct((SEQS, K), jnp.float32),
        scratch_shapes=[
            pltpu.VMEM((close, SEQS, K), jnp.float32),
            pltpu.VMEM((SEQS, K), jnp.float32),
            pltpu.VMEM((wide, SEQS, K), jnp.float32),
            dma((close,)),
            dma((close,)),
            dma((wide,)),
            dma((wide,)),
        ],
        compiler_params=pltpu.CompilerParams(collective_id=1, has_side_effects=True),
        name="reduce",
    )(terms)


def solution(mesh):
    placed = (
        P(("groups", "narrow"), "wide"),
        P(("groups", "wide"), "narrow"),
        P("wide", "narrow"),
        P("groups"),
        P(),
        P("wide"),
        P("narrow"),
    )
    return jax.shard_map(
        on_device, mesh=mesh, in_specs=placed, out_specs=P("groups", None), check_vma=False
    )
```
